256 devices in a mesh: row: 32 (over x, z_hi, core), col: 8 (over y, z_lo).
Axes of the slice: x: 4, y: 4, z: 8 (z_hi: 4, z_lo: 2; z = z_hi * 2 + z_lo), core: 2. Of those that a mesh axis runs over, the one named last changes fastest.
Arguments:
- logits: float32 [8, 4096, 4096], P(None, 'row', 'col'), may hold values from -10 to 303
- values: bfloat16 [8, 4096, 256], P(None, ('col', 'row')), may hold values from -6 to 6
- output_gradient: bfloat16 [8, 4096, 256], P(None, ('col', 'row')), may hold values from -6 to 6
Outputs:
- logit_grad: float32 [8, 4096, 4096], P(None, 'row', 'col')
- value_gradient: bfloat16 [8, 4096, 256], P(None, ('col', 'row'))
The draws below stay inside these ranges and needn't reach their ends.
All inputs are finite; a program needn't handle non-finite values.
Results may differ from the reference program's by a relative error of at most 0.0049.
Values may be sent and summed in bfloat16 or wider, within the bound.
A program may use at most 64 MiB of HBM per device.

```python
import jax
import jax.numpy as jnp
from jax import lax

ATTENTION_HEADS = 8
HEAD_CHANNELS = 32
ALIGNMENT_ROWS = 8
CROP_RESIDUES = 4096
VALUE_FEATURES = 256


def draw_logits(key, part):
    first = jax.random.fold_in(jax.random.fold_in(key, 11), 0)
    fourth = jax.random.fold_in(jax.random.fold_in(key, 11), 3)
    array_dims = (ATTENTION_HEADS, CROP_RESIDUES, CROP_RESIDUES)
    row_scale = jnp.exp(jax.random.uniform(fourth, (ATTENTION_HEADS, CROP_RESIDUES, 1), jnp.float32, -1.0, 1.0))
    base = jnp.clip(2.0 * row_scale * jax.random.normal(first, array_dims, jnp.float32), -10.0, 10.0)
    return base


def block_scale(stream_key, extent, cuts, low, high):
    gain = 1.0
    for dim, blocks in cuts:
        draws = jax.random.uniform(jax.random.fold_in(jax.random.fold_in(stream_key, 6), dim), (blocks,), jnp.float32, low / len(cuts), high / len(cuts))
        gain = gain * jnp.repeat(jnp.exp(draws), extent[dim] // blocks).reshape((-1,) + (1,) * (len(extent) - 1 - dim))
    return gain


def gaussian(stream_key, shape, scale, reach, pieces=(), kind=jnp.bfloat16):
    gain = block_scale(stream_key, shape, pieces, -0.22, 0.18) if pieces else 1.0
    drawn = jax.random.normal(stream_key, shape, jnp.float32) * scale * gain
    return jnp.minimum(jnp.maximum(drawn, -reach), reach).astype(kind)


def setup_inputs(seed: int = 0) -> dict:
    keys = jax.random.split(jax.random.key(seed), 4)
    return {
        "logits": draw_logits(jax.random.fold_in(keys[3], 71), 0),
        "values": gaussian(keys[1], (ALIGNMENT_ROWS, CROP_RESIDUES, VALUE_FEATURES), 1.0, 6.0, ((1, 256),)),
        "output_gradient": gaussian(keys[2], (ALIGNMENT_ROWS, CROP_RESIDUES, VALUE_FEATURES), 1.0, 6.0, ((1, 256),)),
    }


def head_backward(packed):
    head_logits, head_values, head_grads = packed
    top = jnp.max(head_logits, axis=1, keepdims=True)
    exponent = jnp.exp(head_logits - top)
    weights = exponent / jnp.sum(exponent, axis=1, keepdims=True)
    weight_grad = jnp.einsum("sic,sjc->ij", head_grads.astype(jnp.float32), head_values.astype(jnp.float32))
    row_dot = jnp.sum(weights * weight_grad, axis=1, keepdims=True)
    logit_grad = weights * (weight_grad - row_dot)
    weights_half = weights.astype(jnp.bfloat16)
    value_head = jnp.einsum("ij,sic->sjc", weights_half.astype(jnp.float32), head_grads.astype(jnp.float32))
    return logit_grad, value_head


def reference(logits, values, output_gradient):
    alignment_rows = values.shape[0]
    residue_total = values.shape[1]
    value_pieces = values.reshape(alignment_rows, residue_total, ATTENTION_HEADS, HEAD_CHANNELS).transpose(2, 0, 1, 3)
    gradient_pieces = output_gradient.reshape(alignment_rows, residue_total, ATTENTION_HEADS, HEAD_CHANNELS).transpose(2, 0, 1, 3)
    logit_grad, value_head_split = lax.map(head_backward, (logits, value_pieces, gradient_pieces))
    value_gradient = value_head_split.transpose(1, 2, 0, 3).reshape(alignment_rows, residue_total, ATTENTION_HEADS * HEAD_CHANNELS)
    return logit_grad, value_gradient.astype(jnp.bfloat16)
```

```python
import functools

import jax
import jax.numpy as jnp
from jax import lax
from jax.experimental import pallas as pl
from jax.experimental.pallas import tpu as pltpu
from jax.sharding import PartitionSpec as P

RING = 4
HEADS = 8
BLOCK = 16
F32 = jnp.float32
BF16 = jnp.bfloat16


def regroup(pieces, width):
    count = pieces[0].shape[1] // width
    return [
        jnp.concatenate([piece[:, b * width : (b + 1) * width] for piece in pieces], axis=1)
        for b in range(count)
    ]


def kernel(
    logits_ref, values_ref, grads_ref, logit_grad_ref, value_grad_ref,
    vals, ogs, own_grads, wts, wgs, part, core_in, xhalf, xfull, zhalf, zfull,
    stat, dots, load_sem, store_sem, send_sem, recv_sem,
):
    row, col = lax.axis_index("row"), lax.axis_index("col")
    x, zh, k = row // 8, row // 2 % 4, row % 2
    y, zl = col // 2, col % 2

    def at(x=x, zh=zh, k=k, y=y, zl=zl):
        return {"row": (x % 4) * 8 + (zh % 4) * 2 + k, "col": (y % 4) * 2 + zl}

    def slot(dx=0, dz=0):
        return (x + dx + 4) % 4 * 4 + (zh + dz + 4) % 4

    def line(dx=0, dz=0, core=k):
        return slot(dx, dz) * 2 + core

    started = []

    def send(src, dst, where):
        n = len(started)
        copy = pltpu.make_async_remote_copy(
            src_ref=src, dst_ref=dst, send_sem=send_sem.at[n], recv_sem=recv_sem.at[n],
            device_id=where, device_id_type=pl.DeviceIdType.MESH,
        )
        copy.start()
        started.append(copy)
        return copy

    sibling = at(k=1 - k)
    xs = {1: at(x=x + 1), -1: at(x=x + 3)}
    zs = {1: at(zh=zh + 1), -1: at(zh=zh + 3)}
    ys = {1: at(y=y + 1), -1: at(y=y + 3)}
    cols = [{"row": row, "col": (col + d) % 8} for d in range(1, 8)]
    grads_from = at(x=zh % 2 * 2 + k, zh=y + 2, k=zl, y=x, zl=zh // 2)
    grads_to = at(x=y, zh=zl * 2 + x // 2, k=x % 2, y=zh + 2, zl=k)

    loads = []
    for h in range(HEADS):
        load = pltpu.make_async_copy(logits_ref.at[h], wts.at[h], load_sem.at[h])
        load.start()
        loads.append(load)

    barrier = pltpu.get_barrier_semaphore()
    greeted = [sibling, *xs.values(), *zs.values(), *cols, grads_from]
    for device in greeted:
        pl.semaphore_signal(barrier, inc=1, device_id=device, device_id_type=pl.DeviceIdType.MESH)

    for h, piece in enumerate(regroup([grads_ref[s] for s in range(8)], 32)):
        own_grads[h] = piece
    for h, piece in enumerate(regroup([values_ref[s] for s in range(8)], 32)):
        vals[row, h] = piece

    pl.semaphore_wait(barrier, len(greeted))

    piece = zh * 2 + k
    grads_in = send(own_grads, ogs.at[piece], grads_to)

    def share(ref_slot, where, heads=None):
        ref = vals.at[ref_slot] if heads is None else vals.at[ref_slot, pl.ds(heads, 4)]
        return send(ref, ref, where)

    z_first = {d: share(row, zs[d]) for d in (1, -1)}
    x_first = {0: {d: share(row, xs[d]) for d in (1, -1)}}
    core_values = [share(row, sibling)]

    lanes = lax.broadcasted_iota(jnp.int32, (128, 128), 1)
    table = jnp.zeros((128, 128), F32)
    for h in range(HEADS):
        loads[h].wait()
        block = wts[h]
        top = jnp.max(block, axis=1, keepdims=True)
        exponent = jnp.exp(block - top)
        wts[h] = exponent
        table = jnp.where(lanes == h, top, table)
        table = jnp.where(lanes == 8 + h, jnp.sum(exponent, axis=1, keepdims=True), table)
    stat[col] = table.T[:16]
    stat_in = [send(stat.at[col], stat.at[col], device) for device in cols]

    grads_in.wait_recv()
    mine = (col + 4) % 8
    other = (at(zl=1 - zl)["col"] + 4) % 8
    twin_in = send(ogs.at[mine], ogs.at[mine], at(zl=1 - zl))
    y_own = {d: send(ogs.at[mine], ogs.at[mine], ys[d]) for d in (1, -1)}

    def of_y(p, d):
        return (p - 2 * d + 8) % 8

    z_second = {}
    for d in (1, -1):
        z_first[d].wait_recv()
        got = line(dz=-d)
        z_second[d] = share(got, zs[d], 0 if d == 1 else 4)
        x_first[-d] = {e: share(got, xs[e]) for e in (1, -1)}
        core_values.append(share(got, sibling))

    twin_in.wait_recv()
    y_other = {d: send(ogs.at[other], ogs.at[other], ys[d]) for d in (1, -1)}

    x_second = []

    def x_arrivals(dz):
        for d in (1, -1):
            x_first[dz][d].wait_recv()
            got = line(dx=-d, dz=dz)
            x_second.append(share(got, xs[d], 0 if d == 1 else 4))
            core_values.append(share(got, sibling))

    x_arrivals(0)

    y_own[1].wait_recv()
    got = of_y(mine, 1)
    y_second_a = send(ogs.at[got], ogs.at[got], ys[1])
    y_own[-1].wait_recv()

    for copy in z_second.values():
        copy.wait_recv()
    got = line(dz=2)
    x_first[2] = {e: share(got, xs[e]) for e in (1, -1)}
    core_values.append(share(got, sibling))

    y_other[-1].wait_recv()
    got = of_y(other, -1)
    y_second_b = send(ogs.at[got], ogs.at[got], ys[-1])
    y_other[1].wait_recv()

    for copy in stat_in:
        copy.wait_recv()
    tops, sums = stat[:, 0:8, :], stat[:, 8:16, :]
    top = jnp.max(tops, axis=0)
    total = jnp.sum(sums * jnp.exp(tops - top[None]), axis=0)
    factor = jnp.exp(stat[col, 0:8, :] - top) / total
    factor = jnp.concatenate([factor] * 16, axis=0).T

    x_arrivals(-1)
    x_arrivals(1)

    y_second_a.wait_recv()
    y_second_b.wait_recv()

    core_sums = []
    for h in range(HEADS):
        weight = wts[h] * factor[:, h : h + 1]
        wts[h] = weight
        og = ogs[:, h].reshape(128, 256)
        addend = lax.dot_general(
            weight.astype(BF16), og, (((0,), (0,)), ((), ())), preferred_element_type=F32
        ).astype(BF16).reshape(16, 2, BLOCK, 256)
        part[0, h] = addend[:, 0]
        part[1, h] = addend[:, 1]
        core_sums.append(send(part.at[1 - k, h], core_in.at[h], sibling))

    x_arrivals(2)

    for copy in core_sums:
        copy.wait_recv()

    def add_core(s):
        part[k, :, s] = (part[k, :, s].astype(F32) + core_in[:, s].astype(F32)).astype(BF16)

    order = (2, 1, -1, 0)
    half_in = {}
    for dz in order:
        s = slot(2, dz)
        add_core(s)
        for d in (1, -1):
            heads = pl.ds(0 if d == 1 else 4, 4)
            half_in[dz, d] = send(part.at[k, heads, s], xhalf.at[0 if d == 1 else 1, :, slot(0, dz) % 4], xs[d])

    for copy in x_second:
        copy.wait_recv()
    for dz in (0, -1, 1, 2):
        core_values.append(share(line(dx=2, dz=dz), sibling))

    full_in = {}
    for dz in order:
        for d in (1, -1):
            s = slot(d, dz)
            add_core(s)
            half_in[dz, d].wait_recv()
            heads = pl.ds(0 if d == 1 else 4, 4)
            part[k, heads, s] = (
                part[k, heads, s].astype(F32) + xhalf[0 if d == 1 else 1, :, slot(0, dz) % 4].astype(F32)
            ).astype(BF16)
            full_in[dz, d] = send(part.at[k, :, s], xfull.at[0 if d == 1 else 1, :, slot(0, dz) % 4], xs[d])
    for dz in order:
        add_core(slot(0, dz))

    for copy in core_values:
        copy.wait_recv()
    table = jnp.zeros((128, 128), F32)
    for h in range(HEADS):
        weight_grad = lax.dot_general(
            ogs[:, h].reshape(128, 256), vals[:, h].reshape(512, 256),
            (((1,), (1,)), ((), ())), preferred_element_type=F32,
        )
        wgs[h] = weight_grad
        table = jnp.where(lanes == h, jnp.sum(weight_grad * wts[h], axis=1, keepdims=True), table)
    dots[col] = table.T[:8]
    dot_in = [send(dots.at[col], dots.at[col], device) for device in cols]

    def arrived(dz):
        s = slot(0, dz)
        total = part[k, :, s].astype(F32)
        for d in (1, -1):
            full_in[dz, d].wait_recv()
            total += xfull[0 if d == 1 else 1, :, slot(0, dz) % 4].astype(F32)
        return s, total

    s, total = arrived(2)
    part[k, :, s] = total.astype(BF16)
    z_half = {}
    for d in (1, -1):
        heads = pl.ds(0 if d == 1 else 4, 4)
        z_half[d] = send(part.at[k, heads, s], zhalf.at[0 if d == 1 else 1], zs[d])

    for copy in dot_in:
        copy.wait_recv()
    row_dot = jnp.sum(dots[...], axis=0)
    row_dot = jnp.concatenate([row_dot] * 16, axis=0).T
    stores = []
    for h in range(HEADS):
        wgs[h] = wts[h] * (wgs[h] - row_dot[:, h : h + 1])
        store = pltpu.make_async_copy(wgs.at[h], logit_grad_ref.at[h], store_sem.at[h])
        store.start()
        stores.append(store)

    z_full = {}
    for d in (1, -1):
        s, total = arrived(d)
        z_half[d].wait_recv()
        if d == 1:
            part[k, 0:4, s] = (total[0:4] + zhalf[0].astype(F32)).astype(BF16)
            part[k, 4:8, s] = total[4:8].astype(BF16)
        else:
            part[k, 0:4, s] = total[0:4].astype(BF16)
            part[k, 4:8, s] = (total[4:8] + zhalf[1].astype(F32)).astype(BF16)
        z_full[d] = send(part.at[k, :, s], zfull.at[0 if d == 1 else 1], zs[d])
    s, total = arrived(0)
    for d in (1, -1):
        z_full[d].wait_recv()
        total += zfull[0 if d == 1 else 1].astype(F32)
    for s, piece in enumerate(regroup([total[h] for h in range(8)], 32)):
        value_grad_ref[s] = piece.astype(BF16)

    for store in stores:
        store.wait()
    for copy in started:
        copy.wait_send()


def per_device(logits, values, output_gradient):
    vmem = pl.BlockSpec(memory_space=pltpu.VMEM)
    hbm = pl.BlockSpec(memory_space=pl.ANY)
    copies = 112
    return pl.pallas_call(
        kernel,
        out_shape=(
            jax.ShapeDtypeStruct(logits.shape, F32),
            jax.ShapeDtypeStruct(values.shape, BF16),
        ),
        in_specs=[hbm, vmem, vmem],
        out_specs=(hbm, vmem),
        scratch_shapes=[
            pltpu.VMEM((32, HEADS, BLOCK, 256), BF16),
            pltpu.VMEM((8, HEADS, BLOCK, 256), BF16),
            pltpu.VMEM((HEADS, BLOCK, 256), BF16),
            pltpu.VMEM((HEADS, 128, 512), F32),
            pltpu.VMEM((HEADS, 128, 512), F32),
            pltpu.VMEM((2, HEADS, 16, BLOCK, 256), BF16),
            pltpu.VMEM((HEADS, 16, BLOCK, 256), BF16),
            pltpu.VMEM((2, 4, RING, BLOCK, 256), BF16),
            pltpu.VMEM((2, HEADS, RING, BLOCK, 256), BF16),
            pltpu.VMEM((2, 4, BLOCK, 256), BF16),
            pltpu.VMEM((2, HEADS, BLOCK, 256), BF16),
            pltpu.VMEM((8, 16, 128), F32),
            pltpu.VMEM((8, 8, 128), F32),
            pltpu.SemaphoreType.DMA((HEADS,)),
            pltpu.SemaphoreType.DMA((HEADS,)),
            pltpu.SemaphoreType.DMA((copies,)),
            pltpu.SemaphoreType.DMA((copies,)),
        ],
        compiler_params=pltpu.CompilerParams(
            collective_id=0, has_side_effects=True, vmem_limit_bytes=40 * 1024 * 1024
        ),
    )(logits, values, output_gradient)


def solution(mesh):
    placed = (P(None, "row", "col"), P(None, ("col", "row"), None), P(None, ("col", "row"), None))
    return jax.shard_map(
        per_device,
        mesh=mesh,
        in_specs=placed,
        out_specs=(P(None, "row", "col"), P(None, ("col", "row"), None)),
        check_vma=False,
    )
```

```python
import functools

import jax
import jax.numpy as jnp
from jax import lax
from jax.experimental import pallas as pl
from jax.experimental.pallas import tpu as pltpu
from jax.sharding import PartitionSpec as P

RING = 4
HEADS = 8
GROUP = 4
HALF = 2
BLOCK = 16
F32 = jnp.float32
BF16 = jnp.bfloat16


def regroup(pieces, width):
    count = pieces[0].shape[1] // width
    return [
        jnp.concatenate([piece[:, b * width : (b + 1) * width] for piece in pieces], axis=1)
        for b in range(count)
    ]


def kernel(
    logits_ref, values_ref, grads_ref, logit_grad_ref, value_grad_ref,
    raw, vals, ogs, own_grads, wts, wgs, part, core_in, xhalf, xfull, zfull,
    stat, dots, load_sem, send_sem, recv_sem,
):
    row, col = lax.axis_index("row"), lax.axis_index("col")
    x, zh, k = row // 8, row // 2 % 4, row % 2
    y, zl = col // 2, col % 2

    def at(x=x, zh=zh, k=k, y=y, zl=zl):
        return {"row": (x % 4) * 8 + (zh % 4) * 2 + k, "col": (y % 4) * 2 + zl}

    def slot(dx=0, dz=0):
        return (x + dx + 4) % 4 * 4 + (zh + dz + 4) % 4

    def line(dx=0, dz=0, core=k):
        return slot(dx, dz) * 2 + core

    started = []

    def send(src, dst, where):
        n = len(started)
        copy = pltpu.make_async_remote_copy(
            src_ref=src, dst_ref=dst, send_sem=send_sem.at[n], recv_sem=recv_sem.at[n],
            device_id=where, device_id_type=pl.DeviceIdType.MESH,
        )
        copy.start()
        started.append(copy)
        return copy

    sibling = at(k=1 - k)
    xs = {d: at(x=x + d + 4) for d in (1, -1)}
    zs = {d: at(zh=zh + d + 4) for d in (1, -1, 2)}
    ys = {d: at(y=y + d + 4) for d in (1, -1, 2)}
    twin = at(zl=1 - zl)
    cols = [{"row": row, "col": (col + d) % 8} for d in range(1, 8)]
    grads_to = at(x=y, zh=zl * 2 + x // 2, k=x % 2, y=zh, zl=1 - k)
    grads_from = at(x=zh % 2 * 2 + k, zh=y, k=1 - zl, y=x, zl=zh // 2)

    barrier = pltpu.get_barrier_semaphore()
    greeted = [grads_from, *zs.values(), *xs.values(), *cols, sibling]
    for device in greeted:
        pl.semaphore_signal(barrier, inc=1, device_id=device, device_id_type=pl.DeviceIdType.MESH)

    def load(src, dst, n):
        copy = pltpu.make_async_copy(src, dst, load_sem.at[n])
        copy.start()
        loads.append(copy)

    loads = []
    load(grads_ref, raw.at[0], HEADS)
    load(values_ref, raw.at[1], HEADS + 1)
    for h in range(HEADS):
        load(logits_ref.at[h], wts.at[h], h)
    loads[0].wait()
    for h, piece in enumerate(regroup([raw[0, s] for s in range(8)], 32)):
        own_grads[h] = piece
    loads[1].wait()
    for h, piece in enumerate(regroup([raw[1, s] for s in range(8)], 32)):
        vals[row, h] = piece
    loads = loads[2:]

    pl.semaphore_wait(barrier, len(greeted))

    groups = [pl.ds(h, GROUP) for h in range(0, HEADS, GROUP)]

    piece = zh * 2 + k
    grads_in = [send(own_grads.at[heads], ogs.at[piece, heads], grads_to) for heads in groups]

    def share(ref_slot, where, heads=None):
        ref = vals.at[ref_slot] if heads is None else vals.at[ref_slot, pl.ds(heads, 4)]
        return send(ref, ref, where)

    x_first = {0: {d: share(row, xs[d]) for d in (1, -1)}}
    z_first = {d: share(row, zs[d]) for d in (1, -1)}
    z_second = {}
    core_values = [share(row, sibling)]

    lanes = lax.broadcasted_iota(jnp.int32, (128, 128), 1)
    table = jnp.zeros((128, 128), F32)
    for h in range(HEADS):
        loads[h].wait()
        block = wts[h]
        top = jnp.max(block, axis=1, keepdims=True)
        exponent = jnp.exp(block - top)
        wts[h] = exponent
        table = jnp.where(lanes == h, top, table)
        table = jnp.where(lanes == 8 + h, jnp.sum(exponent, axis=1, keepdims=True), table)
    stat[col] = table.T[:16]
    stat_in = [send(stat.at[col], stat.at[col], device) for device in cols]

    mine, other = y * 2 + (1 - zl), y * 2 + zl

    def pass_on(which, heads, where):
        return send(ogs.at[which, heads], ogs.at[which, heads], where)

    twin_in, y_in = [], []
    for g, heads in enumerate(groups):
        grads_in[g].wait_recv()
        twin_in.append(pass_on(mine, heads, twin))
        y_in.append([pass_on(mine, heads, ys[d]) for d in (1, -1, 2)])

    def z_arrival(d):
        got = line(dz=-d)
        if d == 2:
            for copy in z_second.values():
                copy.wait_recv()
        else:
            z_first[d].wait_recv()
            z_second[d] = share(got, zs[d], 0 if d == 1 else 4)
        x_first[2 if d == 2 else -d] = {e: share(got, xs[e]) for e in (1, -1)}
        core_values.append(share(got, sibling))

    x_second = []

    def x_arrivals(dz):
        for d in (1, -1):
            x_first[dz][d].wait_recv()
            got = line(dx=-d, dz=dz)
            x_second.append(share(got, xs[d], 0 if d == 1 else 4))
            core_values.append(share(got, sibling))

    z_arrival(1)
    z_arrival(-1)
    x_arrivals(0)
    for g, heads in enumerate(groups):
        twin_in[g].wait_recv()
        y_in[g] += [pass_on(other, heads, ys[d]) for d in (1, -1, 2)]

    for copy in stat_in:
        copy.wait_recv()
    tops, sums = stat[:, 0:8, :], stat[:, 8:16, :]
    top = jnp.max(tops, axis=0)
    total = jnp.sum(sums * jnp.exp(tops - top[None]), axis=0)
    factor = jnp.exp(stat[col, 0:8, :] - top) / total
    factor = jnp.concatenate([factor] * 16, axis=0).T
    for h in range(HEADS):
        wts[h] = wts[h] * factor[:, h : h + 1]
    z_arrival(2)

    core_sums = []

    def addends(g):
        for copy in y_in[g]:
            copy.wait_recv()
        for h in range(g * GROUP, (g + 1) * GROUP):
            og = ogs[:, h].reshape(128, 256)
            addend = lax.dot_general(
                wts[h].astype(BF16), og, (((0,), (0,)), ((), ())), preferred_element_type=F32
            ).astype(BF16).reshape(16, 2, BLOCK, 256)
            part[0, h] = addend[:, 0]
            part[1, h] = addend[:, 1]
            if h % HALF == HALF - 1:
                heads = pl.ds(h - HALF + 1, HALF)
                core_sums.append(send(part.at[1 - k, heads], core_in.at[heads], sibling))

    order = (2, 1, -1, 0)
    place = {1: 0, -1: 1, 2: 2}

    def half_of(g, d):
        return pl.ds(g * GROUP + (0 if d == 1 else HALF), HALF)

    def zslot(dz):
        return (zh + dz + 4) % 4

    half_in, full_in = {}, {}

    def send_halves(g):
        for d in (1, -1):
            heads = half_of(g, d)
            core_sums[g * 2 + place[d]].wait_recv()
            for dz in order:
                s = slot(2, dz)
                part[k, heads, s] = (part[k, heads, s].astype(F32) + core_in[heads, s].astype(F32)).astype(BF16)
                half_in[g, dz, d] = send(part.at[k, heads, s], xhalf.at[place[d], g, :, zslot(dz)], xs[d])

    def send_fulls(g):
        for dz in order:
            for d in (1, -1):
                s = slot(d, dz)
                heads = half_of(g, -d)
                part[k, heads, s] = (part[k, heads, s].astype(F32) + core_in[heads, s].astype(F32)).astype(BF16)
                half_in[g, dz, d].wait_recv()
                heads = half_of(g, d)
                part[k, heads, s] = (
                    part[k, heads, s].astype(F32) + core_in[heads, s].astype(F32)
                    + xhalf[place[d], g, :, zslot(dz)].astype(F32)
                ).astype(BF16)
                full_in[g, dz, d] = send(
                    part.at[k, groups[g], s], xfull.at[place[d], groups[g], zslot(dz)], xs[d]
                )

    addends(0)
    x_arrivals(1)
    x_arrivals(-1)
    send_halves(0)
    addends(1)
    send_halves(1)

    x_arrivals(2)
    send_fulls(0)
    for copy in x_second[:6]:
        copy.wait_recv()
    for dz in (0, 1, -1):
        core_values.append(share(line(dx=2, dz=dz), sibling))
    send_fulls(1)

    for copy in x_second[6:]:
        copy.wait_recv()
    core_values.append(share(line(dx=2, dz=2), sibling))
    for copy in core_values:
        copy.wait_recv()
    table = jnp.zeros((128, 128), F32)
    for h in range(HEADS):
        weight_grad = lax.dot_general(
            ogs[:, h].reshape(128, 256), vals[:, h].reshape(512, 256),
            (((1,), (1,)), ((), ())), preferred_element_type=F32,
        )
        wgs[h] = weight_grad
        table = jnp.where(lanes == h, jnp.sum(weight_grad * wts[h], axis=1, keepdims=True), table)
    dots[col] = table.T[:8]
    dot_in = [send(dots.at[col], dots.at[col], device) for device in cols]

    def arrived(g, dz):
        s, heads = slot(0, dz), groups[g]
        total = part[k, heads, s].astype(F32) + core_in[heads, s].astype(F32)
        for d in (1, -1):
            full_in[g, dz, d].wait_recv()
            total += xfull[place[d], heads, zslot(dz)].astype(F32)
        return s, total

    z_full = {}
    for g, heads in enumerate(groups):
        for dz in (2, 1, -1):
            s, total = arrived(g, dz)
            part[k, heads, s] = total.astype(BF16)
            z_full[g, dz] = send(part.at[k, heads, s], zfull.at[place[dz], heads], zs[dz])

    for copy in dot_in:
        copy.wait_recv()
    row_dot = jnp.sum(dots[...], axis=0)
    row_dot = jnp.concatenate([row_dot] * 16, axis=0).T
    for h in range(HEADS):
        logit_grad_ref[h] = wts[h] * (wgs[h] - row_dot[:, h : h + 1])

    totals = []
    for g, heads in enumerate(groups):
        s, total = arrived(g, 0)
        for dz in (2, 1, -1):
            z_full[g, dz].wait_recv()
            total += zfull[place[dz], heads].astype(F32)
        totals += [total[h] for h in range(GROUP)]
    for s, piece in enumerate(regroup(totals, 32)):
        value_grad_ref[s] = piece.astype(BF16)

    for copy in started:
        copy.wait_send()


def store(logit_grad, value_grad, logit_grad_ref, value_grad_ref, sem):
    copies = [
        pltpu.make_async_copy(logit_grad, logit_grad_ref, sem.at[0]),
        pltpu.make_async_copy(value_grad, value_grad_ref, sem.at[1]),
    ]
    for copy in copies:
        copy.start()
    for copy in copies:
        copy.wait()


def per_device(logits, values, output_gradient):
    vmem = pl.BlockSpec(memory_space=pltpu.VMEM)
    hbm = pl.BlockSpec(memory_space=pltpu.HBM)
    copies = 136
    outs = (jax.ShapeDtypeStruct(logits.shape, F32), jax.ShapeDtypeStruct(values.shape, BF16))
    results = pl.pallas_call(
        kernel,
        out_shape=outs,
        in_specs=[hbm] * 3,
        out_specs=(vmem, vmem),
        scratch_shapes=[
            pltpu.VMEM((2, 8, BLOCK, 256), BF16),
            pltpu.VMEM((32, HEADS, BLOCK, 256), BF16),
            pltpu.VMEM((8, HEADS, BLOCK, 256), BF16),
            pltpu.VMEM((HEADS, BLOCK, 256), BF16),
            pltpu.VMEM((HEADS, 128, 512), F32),
            pltpu.VMEM((HEADS, 128, 512), F32),
            pltpu.VMEM((2, HEADS, 16, BLOCK, 256), BF16),
            pltpu.VMEM((HEADS, 16, BLOCK, 256), BF16),
            pltpu.VMEM((2, HEADS // GROUP, HALF, RING, BLOCK, 256), BF16),
            pltpu.VMEM((2, HEADS, RING, BLOCK, 256), BF16),
            pltpu.VMEM((3, HEADS, BLOCK, 256), BF16),
            pltpu.VMEM((8, 16, 128), F32),
            pltpu.VMEM((8, 8, 128), F32),
            pltpu.SemaphoreType.DMA((HEADS + 2,)),
            pltpu.SemaphoreType.DMA((copies,)),
            pltpu.SemaphoreType.DMA((copies,)),
        ],
        compiler_params=pltpu.CompilerParams(
            collective_id=0, has_side_effects=True, vmem_limit_bytes=52224 * 1024
        ),
    )(logits, values, output_gradient)
    return pl.pallas_call(
        store,
        out_shape=outs,
        in_specs=[pl.BlockSpec(memory_space=pl.ANY)] * 2,
        out_specs=(hbm, hbm),
        scratch_shapes=[pltpu.SemaphoreType.DMA((2,))],
        compiler_params=pltpu.CompilerParams(vmem_limit_bytes=1024 * 1024),
    )(*results)


def solution(mesh):
    placed = (P(None, "row", "col"), P(None, ("col", "row"), None), P(None, ("col", "row"), None))
    return jax.shard_map(
        per_device,
        mesh=mesh,
        in_specs=placed,
        out_specs=(P(None, "row", "col"), P(None, ("col", "row"), None)),
        check_vma=False,
    )
```

```python
import functools

import jax
import jax.numpy as jnp
from jax import lax
from jax.experimental import pallas as pl
from jax.experimental.pallas import tpu as pltpu
from jax.sharding import PartitionSpec as P

RING = 4
HEADS = 8
GROUP = 4
HALF = 2
BLOCK = 16
F32 = jnp.float32
BF16 = jnp.bfloat16


def regroup(pieces, width):
    count = pieces[0].shape[1] // width
    return [
        jnp.concatenate([piece[:, b * width : (b + 1) * width] for piece in pieces], axis=1)
        for b in range(count)
    ]


def kernel(
    logits_ref, values_ref, grads_ref, logit_grad_ref, value_grad_ref,
    raw, vals, ogs, own_grads, wts, wgs, part, core_in, xhalf, xfull, zfull,
    stat, dots, load_sem, send_sem, recv_sem,
):
    row, col = lax.axis_index("row"), lax.axis_index("col")
    x, zh, k = row // 8, row // 2 % 4, row % 2
    y, zl = col // 2, col % 2

    def at(x=x, zh=zh, k=k, y=y, zl=zl):
        return {"row": (x % 4) * 8 + (zh % 4) * 2 + k, "col": (y % 4) * 2 + zl}

    def slot(dx=0, dz=0):
        return (x + dx + 4) % 4 * 4 + (zh + dz + 4) % 4

    def slots(dx):
        return pl.ds((x + dx + 4) % 4 * 4, 4)

    started = []

    def send(src, dst, where):
        n = len(started)
        copy = pltpu.make_async_remote_copy(
            src_ref=src, dst_ref=dst, send_sem=send_sem.at[n], recv_sem=recv_sem.at[n],
            device_id=where, device_id_type=pl.DeviceIdType.MESH,
        )
        copy.start()
        started.append(copy)
        return copy

    sibling = at(k=1 - k)
    xs = {d: at(x=x + d + 4) for d in (1, -1)}
    zs = {d: at(zh=zh + d + 4) for d in (1, -1, 2)}
    ys = {d: at(y=y + d + 4) for d in (1, -1, 2)}
    twin = at(zl=1 - zl)
    cols = [{"row": row, "col": (col + d) % 8} for d in range(1, 8)]
    grads_to = at(x=y, zh=zl * 2 + x // 2, k=x % 2, y=zh, zl=1 - k)
    grads_from = at(x=zh % 2 * 2 + k, zh=y, k=1 - zl, y=x, zl=zh // 2)

    barrier = pltpu.get_barrier_semaphore()
    greeted = [grads_from, *zs.values(), *xs.values(), *cols, sibling]
    for device in greeted:
        pl.semaphore_signal(barrier, inc=1, device_id=device, device_id_type=pl.DeviceIdType.MESH)

    def load(src, dst, n):
        copy = pltpu.make_async_copy(src, dst, load_sem.at[n])
        copy.start()
        loads.append(copy)

    loads = []
    load(grads_ref, raw.at[0], HEADS)
    load(values_ref, raw.at[1], HEADS + 1)
    for h in range(HEADS):
        load(logits_ref.at[h], wts.at[h], h)
    loads[0].wait()
    for h, piece in enumerate(regroup([raw[0, s] for s in range(8)], 32)):
        own_grads[h] = piece
    loads[1].wait()
    for h, piece in enumerate(regroup([raw[1, s] for s in range(8)], 32)):
        vals[slot(), k, h] = piece
    loads = loads[2:]

    pl.semaphore_wait(barrier, len(greeted))

    groups = [pl.ds(h, GROUP) for h in range(0, HEADS, GROUP)]

    piece = zh * 2 + k
    grads_in = [send(own_grads.at[heads], ogs.at[piece, heads], grads_to) for heads in groups]

    def share(ref_slot, where, heads=None):
        ref = vals.at[ref_slot, k] if heads is None else vals.at[ref_slot, k, pl.ds(heads, 4)]
        return send(ref, ref, where)

    x_first = {0: {d: share(slot(), xs[d]) for d in (1, -1)}}
    z_first = {d: share(slot(), zs[d]) for d in (1, -1)}
    z_second = {}
    core_values = []

    lanes = lax.broadcasted_iota(jnp.int32, (128, 128), 1)
    table = jnp.zeros((128, 128), F32)

    def column(wide, h):
        return jnp.sum(jnp.where(lanes == h, wide, 0.0), axis=1, keepdims=True)

    def head_stats(h, table):
        block = wts[h]
        top = jnp.max(block, axis=1, keepdims=True)
        exponent = jnp.exp(block - top)
        wts[h] = exponent
        table = jnp.where(lanes == h, top, table)
        return jnp.where(lanes == 8 + h, jnp.sum(exponent, axis=1, keepdims=True), table)

    for load in loads:
        load.wait()
    table = lax.fori_loop(0, HEADS, head_stats, table)
    stat[col] = table.T[:16]
    stat_in = [send(stat.at[col], stat.at[col], device) for device in cols]

    mine, other = y * 2 + (1 - zl), y * 2 + zl

    def pass_on(which, heads, where):
        return send(ogs.at[which, heads], ogs.at[which, heads], where)

    twin_in, y_in = [], []
    for g, heads in enumerate(groups):
        grads_in[g].wait_recv()
        twin_in.append(pass_on(mine, heads, twin))
        y_in.append([pass_on(mine, heads, ys[d]) for d in (1, -1, 2)])

    def z_arrival(d):
        got = slot(dz=-d)
        if d == 2:
            for copy in z_second.values():
                copy.wait_recv()
        else:
            z_first[d].wait_recv()
            z_second[d] = share(got, zs[d], 0 if d == 1 else 4)
        x_first[2 if d == 2 else -d] = {e: share(got, xs[e]) for e in (1, -1)}

    x_second = []

    def share_core(dx):
        core_values.append(send(vals.at[slots(dx), k], vals.at[slots(dx), k], sibling))

    def x_arrivals(dz):
        for d in (1, -1):
            x_first[dz][d].wait_recv()
            got = slot(dx=-d, dz=dz)
            x_second.append(share(got, xs[d], 0 if d == 1 else 4))

    z_arrival(1)
    z_arrival(-1)
    x_arrivals(0)
    for g, heads in enumerate(groups):
        twin_in[g].wait_recv()
        y_in[g] += [pass_on(other, heads, ys[d]) for d in (1, -1, 2)]

    for copy in stat_in:
        copy.wait_recv()
    tops, sums = stat[:, 0:8, :], stat[:, 8:16, :]
    top = jnp.max(tops, axis=0)
    total = jnp.sum(sums * jnp.exp(tops - top[None]), axis=0)
    factor = jnp.exp(stat[col, 0:8, :] - top) / total
    factor = jnp.concatenate([factor] * 16, axis=0).T

    def scale(h, carry):
        wts[h] = wts[h] * column(factor, h)
        return carry

    lax.fori_loop(0, HEADS, scale, 0)
    z_arrival(2)
    share_core(0)

    core_sums = []

    def addend_of(h, carry):
        og = ogs[:, h].reshape(128, 256)
        addend = lax.dot_general(
            wts[h].astype(BF16), og, (((0,), (0,)), ((), ())), preferred_element_type=F32
        ).astype(BF16).reshape(16, 2, BLOCK, 256)
        part[0, h] = addend[:, 0]
        part[1, h] = addend[:, 1]
        return carry

    def addends(g):
        for copy in y_in[g]:
            copy.wait_recv()
        for start in range(g * GROUP, (g + 1) * GROUP, HALF):
            lax.fori_loop(start, start + HALF, addend_of, 0)
            heads = pl.ds(start, HALF)
            core_sums.append(send(part.at[1 - k, heads], core_in.at[heads], sibling))

    order = (2, 1, -1, 0)
    place = {1: 0, -1: 1, 2: 2}

    def half_of(g, d):
        return pl.ds(g * GROUP + (0 if d == 1 else HALF), HALF)

    def zslot(dz):
        return (zh + dz + 4) % 4

    half_in, full_in = {}, {}

    def send_halves(g):
        for d in (1, -1):
            heads, there = half_of(g, d), slots(2)
            core_sums[g * 2 + place[d]].wait_recv()
            part[k, heads, there] = (
                part[k, heads, there].astype(F32) + core_in[heads, there].astype(F32)
            ).astype(BF16)
            half_in[g, d] = send(part.at[k, heads, there], xhalf.at[place[d], g], xs[d])

    def send_fulls(g):
        for d in (1, -1):
            heads, there = half_of(g, -d), slots(d)
            part[k, heads, there] = (
                part[k, heads, there].astype(F32) + core_in[heads, there].astype(F32)
            ).astype(BF16)
        for d in (1, -1):
            heads, there = half_of(g, d), slots(d)
            half_in[g, d].wait_recv()
            part[k, heads, there] = (
                part[k, heads, there].astype(F32) + core_in[heads, there].astype(F32)
                + xhalf[place[d], g].astype(F32)
            ).astype(BF16)
            for dz in order:
                full_in[g, dz, d] = send(
                    part.at[k, groups[g], slot(d, dz)], xfull.at[place[d], groups[g], zslot(dz)], xs[d]
                )

    def arrived(g, dz):
        s, heads = slot(0, dz), groups[g]
        total = part[k, heads, s].astype(F32) + core_in[heads, s].astype(F32)
        for d in (1, -1):
            full_in[g, dz, d].wait_recv()
            total += xfull[place[d], heads, zslot(dz)].astype(F32)
        return s, total

    z_full = {}

    def send_on(g):
        heads = groups[g]
        for dz in (2, 1, -1):
            s, total = arrived(g, dz)
            part[k, heads, s] = total.astype(BF16)
            z_full[g, dz] = send(part.at[k, heads, s], zfull.at[place[dz], heads], zs[dz])

    x_arrivals(1)
    x_arrivals(-1)
    addends(0)
    send_halves(0)
    addends(1)
    send_halves(1)

    x_arrivals(2)
    share_core(1)
    share_core(-1)
    send_fulls(0)
    send_fulls(1)
    send_on(0)

    for copy in x_second:
        copy.wait_recv()
    share_core(2)
    for copy in core_values:
        copy.wait_recv()
    table = jnp.zeros((128, 128), F32)

    def weight_grads(h, table):
        weight_grad = lax.dot_general(
            ogs[:, h].reshape(128, 256), vals[:, :, h].reshape(512, 256),
            (((1,), (1,)), ((), ())), preferred_element_type=F32,
        )
        wgs[h] = weight_grad
        return jnp.where(lanes == h, jnp.sum(weight_grad * wts[h], axis=1, keepdims=True), table)

    for h in range(HEADS):
        table = weight_grads(h, table)
    dots[col] = table.T[:8]
    dot_in = [send(dots.at[col], dots.at[col], device) for device in cols]

    send_on(1)

    for copy in dot_in:
        copy.wait_recv()
    row_dot = jnp.sum(dots[...], axis=0)
    row_dot = jnp.concatenate([row_dot] * 16, axis=0).T

    for h in range(HEADS):
        logit_grad_ref[h] = wts[h] * (wgs[h] - row_dot[:, h : h + 1])

    totals = []
    for g, heads in enumerate(groups):
        s, total = arrived(g, 0)
        for dz in (2, 1, -1):
            z_full[g, dz].wait_recv()
            total += zfull[place[dz], heads].astype(F32)
        totals += [total[h] for h in range(GROUP)]
    for s, piece in enumerate(regroup(totals, 32)):
        value_grad_ref[s] = piece.astype(BF16)

    for copy in started:
        copy.wait_send()


def store(logit_grad, value_grad, logit_grad_ref, value_grad_ref, sem):
    copies = [
        pltpu.make_async_copy(logit_grad, logit_grad_ref, sem.at[0]),
        pltpu.make_async_copy(value_grad, value_grad_ref, sem.at[1]),
    ]
    for copy in copies:
        copy.start()
    for copy in copies:
        copy.wait()


def per_device(logits, values, output_gradient):
    vmem = pl.BlockSpec(memory_space=pltpu.VMEM)
    hbm = pl.BlockSpec(memory_space=pltpu.HBM)
    copies = 136
    outs = (jax.ShapeDtypeStruct(logits.shape, F32), jax.ShapeDtypeStruct(values.shape, BF16))
    results = pl.pallas_call(
        kernel,
        out_shape=outs,
        in_specs=[hbm] * 3,
        out_specs=(vmem, vmem),
        scratch_shapes=[
            pltpu.VMEM((2, 8, BLOCK, 256), BF16),
            pltpu.VMEM((16, 2, HEADS, BLOCK, 256), BF16),
            pltpu.VMEM((8, HEADS, BLOCK, 256), BF16),
            pltpu.VMEM((HEADS, BLOCK, 256), BF16),
            pltpu.VMEM((HEADS, 128, 512), F32),
            pltpu.VMEM((HEADS, 128, 512), F32),
            pltpu.VMEM((2, HEADS, 16, BLOCK, 256), BF16),
            pltpu.VMEM((HEADS, 16, BLOCK, 256), BF16),
            pltpu.VMEM((2, HEADS // GROUP, HALF, RING, BLOCK, 256), BF16),
            pltpu.VMEM((2, HEADS, RING, BLOCK, 256), BF16),
            pltpu.VMEM((3, HEADS, BLOCK, 256), BF16),
            pltpu.VMEM((8, 16, 128), F32),
            pltpu.VMEM((8, 8, 128), F32),
            pltpu.SemaphoreType.DMA((HEADS + 2,)),
            pltpu.SemaphoreType.DMA((copies,)),
            pltpu.SemaphoreType.DMA((copies,)),
        ],
        compiler_params=pltpu.CompilerParams(
            collective_id=0, has_side_effects=True, vmem_limit_bytes=40 * 1024 * 1024
        ),
    )(*(pltpu.with_memory_space_constraint(a, pltpu.HBM) for a in (logits, values, output_gradient)))
    return pl.pallas_call(
        store,
        out_shape=outs,
        in_specs=[pl.BlockSpec(memory_space=pl.ANY)] * 2,
        out_specs=(hbm, hbm),
        scratch_shapes=[pltpu.SemaphoreType.DMA((2,))],
        compiler_params=pltpu.CompilerParams(vmem_limit_bytes=1024 * 1024),
    )(*results)


def solution(mesh):
    placed = (P(None, "row", "col"), P(None, ("col", "row"), None), P(None, ("col", "row"), None))
    return jax.shard_map(
        per_device,
        mesh=mesh,
        in_specs=placed,
        out_specs=(P(None, "row", "col"), P(None, ("col", "row"), None)),
        check_vma=False,
    )
```

```python
import functools

import jax
import jax.numpy as jnp
from jax import lax
from jax.experimental import pallas as pl
from jax.experimental.pallas import tpu as pltpu
from jax.sharding import PartitionSpec as P

RING = 4
HEADS = 8
GROUP = 4
BLOCK = 16
F32 = jnp.float32
BF16 = jnp.bfloat16


def regroup(pieces, width):
    count = pieces[0].shape[1] // width
    return [
        jnp.concatenate([piece[:, b * width : (b + 1) * width] for piece in pieces], axis=1)
        for b in range(count)
    ]


def kernel(
    logits_ref, values_ref, grads_ref, logit_grad_ref, value_grad_ref,
    raw, vals, ogs, own_grads, wts, wgs, part, core_in, xhalf, xfull, zfull, zearly, early_sum, xlate,
    stat, dots, load_sem, send_sem, recv_sem,
):
    row, col = lax.axis_index("row"), lax.axis_index("col")
    x, zh, k = row // 8, row // 2 % 4, row % 2
    y, zl = col // 2, col % 2

    def at(x=x, zh=zh, k=k, y=y, zl=zl):
        return {"row": (x % 4) * 8 + (zh % 4) * 2 + k, "col": (y % 4) * 2 + zl}

    def slot(dx=0, dz=0):
        return (x + dx + 4) % 4 * 4 + (zh + dz + 4) % 4

    def slots(dx):
        return pl.ds((x + dx + 4) % 4 * 4, 4)

    started = []

    def send(src, dst, where):
        n = len(started)
        copy = pltpu.make_async_remote_copy(
            src_ref=src, dst_ref=dst, send_sem=send_sem.at[n], recv_sem=recv_sem.at[n],
            device_id=where, device_id_type=pl.DeviceIdType.MESH,
        )
        copy.start()
        started.append(copy)
        return copy

    sibling = at(k=1 - k)
    xs = {d: at(x=x + d + 4) for d in (1, -1, 2)}
    zs = {d: at(zh=zh + d + 4) for d in (1, -1, 2)}
    ys = {d: at(y=y + d + 4) for d in (1, -1, 2)}
    twin = at(zl=1 - zl)
    cols = [{"row": row, "col": (col + d) % 8} for d in range(1, 8)]
    grads_to = at(x=y, zh=zl * 2 + x // 2, k=x % 2, y=zh, zl=1 - k)
    grads_from = at(x=zh % 2 * 2 + k, zh=y, k=1 - zl, y=x, zl=zh // 2)

    barrier = pltpu.get_barrier_semaphore()
    greeted = [grads_from, *zs.values(), *xs.values(), *cols, sibling]
    for device in greeted:
        pl.semaphore_signal(barrier, inc=1, device_id=device, device_id_type=pl.DeviceIdType.MESH)

    def load(src, dst, n):
        copy = pltpu.make_async_copy(src, dst, load_sem.at[n])
        copy.start()
        loads.append(copy)

    loads = []
    load(grads_ref, raw.at[0], HEADS)
    load(values_ref, raw.at[1], HEADS + 1)
    for h in range(HEADS):
        load(logits_ref.at[h], wts.at[h], h)
    loads[0].wait()
    for h, piece in enumerate(regroup([raw[0, s] for s in range(8)], 32)):
        own_grads[h] = piece
    loads[1].wait()
    for h, piece in enumerate(regroup([raw[1, s] for s in range(8)], 32)):
        vals[slot(), k, h] = piece
    loads = loads[2:]

    pl.semaphore_wait(barrier, len(greeted))

    groups = [pl.ds(h, GROUP) for h in range(0, HEADS, GROUP)]

    piece = zh * 2 + k
    grads_in = [send(own_grads.at[heads], ogs.at[piece, heads], grads_to) for heads in groups]

    def share(ref_slot, where, heads=None):
        ref = vals.at[ref_slot, k] if heads is None else vals.at[ref_slot, k, pl.ds(heads, 4)]
        return send(ref, ref, where)

    x_first = {0: {d: share(slot(), xs[d]) for d in (1, -1)}}
    z_first = {d: share(slot(), zs[d]) for d in (1, -1)}
    z_second = {}
    core_values = []

    lanes = lax.broadcasted_iota(jnp.int32, (128, 128), 1)
    table = jnp.zeros((128, 128), F32)

    def column(wide, h):
        return jnp.sum(jnp.where(lanes == h, wide, 0.0), axis=1, keepdims=True)

    def head_stats(h, table):
        block = wts[h]
        top = jnp.max(block, axis=1, keepdims=True)
        exponent = jnp.exp(block - top)
        wts[h] = exponent
        table = jnp.where(lanes == h, top, table)
        return jnp.where(lanes == 8 + h, jnp.sum(exponent, axis=1, keepdims=True), table)

    for load in loads:
        load.wait()
    table = lax.fori_loop(0, HEADS, head_stats, table)
    stat[col] = table.T[:16]
    stat_in = [send(stat.at[col], stat.at[col], device) for device in cols]

    mine, other = y * 2 + (1 - zl), y * 2 + zl

    def pass_on(which, heads, where):
        return send(ogs.at[which, heads], ogs.at[which, heads], where)

    twin_in, y_in = [], []
    for g, heads in enumerate(groups):
        grads_in[g].wait_recv()
        twin_in.append(pass_on(mine, heads, twin))
        y_in.append([pass_on(mine, heads, ys[d]) for d in (1, -1, 2)])

    def z_arrival(d):
        got = slot(dz=-d)
        if d == 2:
            for copy in z_second.values():
                copy.wait_recv()
        else:
            z_first[d].wait_recv()
            z_second[d] = share(got, zs[d], 0 if d == 1 else 4)
        x_first[2 if d == 2 else -d] = {e: share(got, xs[e]) for e in (1, -1)}

    x_second = []

    def share_core(dx):
        core_values.append(send(vals.at[slots(dx), k], vals.at[slots(dx), k], sibling))

    def x_arrivals(dz):
        for d in (1, -1):
            x_first[dz][d].wait_recv()
            got = slot(dx=-d, dz=dz)
            x_second.append(share(got, xs[d], 0 if d == 1 else 4))

    z_arrival(1)
    z_arrival(-1)
    x_arrivals(0)
    for g, heads in enumerate(groups):
        twin_in[g].wait_recv()
        y_in[g] += [pass_on(other, heads, ys[d]) for d in (1, -1, 2)]

    for copy in stat_in:
        copy.wait_recv()
    tops, sums = stat[:, 0:8, :], stat[:, 8:16, :]
    top = jnp.max(tops, axis=0)
    total = jnp.sum(sums * jnp.exp(tops - top[None]), axis=0)
    factor = jnp.exp(stat[col, 0:8, :] - top) / total
    factor = jnp.concatenate([factor] * 16, axis=0).T

    def scale(h, carry):
        wts[h] = wts[h] * column(factor, h)
        return carry

    lax.fori_loop(0, HEADS, scale, 0)
    z_arrival(2)
    share_core(0)


    def addend_of(h, carry):
        og = ogs[:, h].reshape(128, 256)
        addend = lax.dot_general(
            wts[h].astype(BF16), og, (((0,), (0,)), ((), ())), preferred_element_type=F32
        ).astype(BF16).reshape(4, 4, 2, BLOCK, 256)
        part[0, h] = addend[:, :, 0]
        part[1, h] = addend[:, :, 1]
        return carry

    core_sums = {}

    def addends(start, count):
        lax.fori_loop(start, start + count, addend_of, 0)
        heads = pl.ds(start, count)
        core_sums[start] = send(part.at[1 - k, heads], core_in.at[heads], sibling)

    order = (2, 1, -1, 0)
    place = {1: 0, -1: 1, 2: 2}
    first, second = (2, 1), (4, 2)

    def heads_of(group):
        return pl.ds(group[0], 2 * group[1])

    def half_of(group, d):
        return pl.ds(group[0] + (0 if d == 1 else group[1]), group[1])

    def held(group, d):
        return xhalf.at[place[d], pl.ds(group[0] // 2, group[1])]

    def plane(dx):
        return (x + dx + 4) % 4

    def zslot(dz):
        return (zh + dz + 4) % 4

    half_in, full_in = {}, {}

    def send_halves(group):
        for d in (1, -1):
            heads, there = half_of(group, d), plane(2)
            core_sums[half_start(group, d)].wait_recv()
            part[k, heads, there] = (
                part[k, heads, there].astype(F32) + core_in[heads, there].astype(F32)
            ).astype(BF16)
            half_in[group, d] = send(part.at[k, heads, there], held(group, d), xs[d])

    def half_start(group, d):
        return group[0] + (0 if d == 1 else group[1])

    def send_fulls(group):
        for d in (1, -1):
            heads, there = half_of(group, -d), plane(d)
            part[k, heads, there] = (
                part[k, heads, there].astype(F32) + core_in[heads, there].astype(F32)
            ).astype(BF16)
        for d in (1, -1):
            heads, there = half_of(group, d), plane(d)
            half_in[group, d].wait_recv()
            part[k, heads, there] = (
                part[k, heads, there].astype(F32) + core_in[heads, there].astype(F32)
                + held(group, d)[...].astype(F32)
            ).astype(BF16)
            for dz in order:
                full_in[group, dz, d] = send(
                    part.at[k, heads_of(group), there, zslot(dz)],
                    xfull.at[place[d], heads_of(group), zslot(dz)], xs[d],
                )

    def arrived(group, dz):
        heads, here = heads_of(group), zslot(dz)
        total = part[k, heads, x, here].astype(F32) + core_in[heads, x, here].astype(F32)
        for d in (1, -1):
            full_in[group, dz, d].wait_recv()
            total += xfull[place[d], heads, here].astype(F32)
        return total

    z_full = {}

    def send_on(group):
        heads = heads_of(group)
        for dz in (2, 1, -1):
            here = zslot(dz)
            part[k, heads, x, here] = arrived(group, dz).astype(BF16)
            z_full[group, dz] = send(part.at[k, heads, x, here], zfull.at[place[dz], heads], zs[dz])

    z_early, x_late = {}, {}

    def send_early():
        heads = pl.ds(0, 2)
        core_sums[0].wait_recv()
        for dz in (2, 1, -1):
            here = zslot(dz)
            part[k, heads, :, here] = (
                part[k, heads, :, here].astype(F32) + core_in[heads, :, here].astype(F32)
            ).astype(BF16)
            z_early[dz] = send(part.at[k, heads, :, here], zearly.at[place[dz]], zs[dz])

    def send_late():
        heads = pl.ds(0, 2)
        total = part[k, heads, :, zh].astype(F32) + core_in[heads, :, zh].astype(F32)
        for dz in (2, 1, -1):
            z_early[dz].wait_recv()
            total += zearly[place[dz]].astype(F32)
        early_sum[...] = total.astype(BF16)
        for dx in (2, 1, -1):
            x_late[dx] = send(early_sum.at[:, plane(dx)], xlate.at[place[dx]], xs[dx])

    x_arrivals(1)
    x_arrivals(-1)
    for copy in y_in[0]:
        copy.wait_recv()
    addends(2, 1)
    addends(3, 1)
    addends(0, 2)
    send_halves(first)
    send_early()
    for copy in y_in[1]:
        copy.wait_recv()
    addends(4, 2)
    addends(6, 2)
    send_halves(second)

    x_arrivals(2)
    share_core(1)
    share_core(-1)
    send_fulls(first)
    send_fulls(second)
    send_on(first)

    for copy in x_second:
        copy.wait_recv()
    share_core(2)
    for copy in core_values:
        copy.wait_recv()
    table = jnp.zeros((128, 128), F32)

    def weight_grads(h, table):
        weight_grad = lax.dot_general(
            ogs[:, h].reshape(128, 256), vals[:, :, h].reshape(512, 256),
            (((1,), (1,)), ((), ())), preferred_element_type=F32,
        )
        wgs[h] = weight_grad
        return jnp.where(lanes == h, jnp.sum(weight_grad * wts[h], axis=1, keepdims=True), table)

    for h in range(HEADS):
        table = weight_grads(h, table)
    dots[col] = table.T[:8]
    dot_in = [send(dots.at[col], dots.at[col], device) for device in cols]
    send_late()

    send_on(second)

    for copy in dot_in:
        copy.wait_recv()
    row_dot = jnp.sum(dots[...], axis=0)
    row_dot = jnp.concatenate([row_dot] * 16, axis=0).T

    for h in range(HEADS):
        logit_grad_ref[h] = wts[h] * (wgs[h] - row_dot[:, h : h + 1])

    early = early_sum[:, x].astype(F32)
    for dx in (2, 1, -1):
        x_late[dx].wait_recv()
        early += xlate[place[dx]].astype(F32)
    totals = [early[0], early[1]]
    for group in (first, second):
        total = arrived(group, 0)
        for dz in (2, 1, -1):
            z_full[group, dz].wait_recv()
            total += zfull[place[dz], heads_of(group)].astype(F32)
        totals += [total[h] for h in range(2 * group[1])]
    for s, piece in enumerate(regroup(totals, 32)):
        value_grad_ref[s] = piece.astype(BF16)

    for copy in started:
        copy.wait_send()


def store(logit_grad, value_grad, logit_grad_ref, value_grad_ref, sem):
    copies = [
        pltpu.make_async_copy(logit_grad, logit_grad_ref, sem.at[0]),
        pltpu.make_async_copy(value_grad, value_grad_ref, sem.at[1]),
    ]
    for copy in copies:
        copy.start()
    for copy in copies:
        copy.wait()


def per_device(logits, values, output_gradient):
    vmem = pl.BlockSpec(memory_space=pltpu.VMEM)
    hbm = pl.BlockSpec(memory_space=pltpu.HBM)
    copies = 136
    outs = (jax.ShapeDtypeStruct(logits.shape, F32), jax.ShapeDtypeStruct(values.shape, BF16))
    results = pl.pallas_call(
        kernel,
        out_shape=outs,
        in_specs=[hbm] * 3,
        out_specs=(vmem, vmem),
        scratch_shapes=[
            pltpu.VMEM((2, 8, BLOCK, 256), BF16),
            pltpu.VMEM((16, 2, HEADS, BLOCK, 256), BF16),
            pltpu.VMEM((8, HEADS, BLOCK, 256), BF16),
            pltpu.VMEM((HEADS, BLOCK, 256), BF16),
            pltpu.VMEM((HEADS, 128, 512), F32),
            pltpu.VMEM((HEADS, 128, 512), F32),
            pltpu.VMEM((2, HEADS, RING, RING, BLOCK, 256), BF16),
            pltpu.VMEM((HEADS, RING, RING, BLOCK, 256), BF16),
            pltpu.VMEM((2, 4, RING, BLOCK, 256), BF16),
            pltpu.VMEM((2, HEADS, RING, BLOCK, 256), BF16),
            pltpu.VMEM((3, HEADS, BLOCK, 256), BF16),
            pltpu.VMEM((3, 2, RING, BLOCK, 256), BF16),
            pltpu.VMEM((2, RING, BLOCK, 256), BF16),
            pltpu.VMEM((3, 2, BLOCK, 256), BF16),
            pltpu.VMEM((8, 16, 128), F32),
            pltpu.VMEM((8, 8, 128), F32),
            pltpu.SemaphoreType.DMA((HEADS + 2,)),
            pltpu.SemaphoreType.DMA((copies,)),
            pltpu.SemaphoreType.DMA((copies,)),
        ],
        compiler_params=pltpu.CompilerParams(
            collective_id=0, has_side_effects=True, vmem_limit_bytes=40 * 1024 * 1024
        ),
    )(*(pltpu.with_memory_space_constraint(a, pltpu.HBM) for a in (logits, values, output_gradient)))
    return pl.pallas_call(
        store,
        out_shape=outs,
        in_specs=[pl.BlockSpec(memory_space=pl.ANY)] * 2,
        out_specs=(hbm, hbm),
        scratch_shapes=[pltpu.SemaphoreType.DMA((2,))],
        compiler_params=pltpu.CompilerParams(vmem_limit_bytes=1024 * 1024),
    )(*results)


def solution(mesh):
    placed = (P(None, "row", "col"), P(None, ("col", "row"), None), P(None, ("col", "row"), None))
    return jax.shard_map(
        per_device,
        mesh=mesh,
        in_specs=placed,
        out_specs=(P(None, "row", "col"), P(None, ("col", "row"), None)),
        check_vma=False,
    )
```

```python
import functools

import jax
import jax.numpy as jnp
from jax import lax
from jax.experimental import pallas as pl
from jax.experimental.pallas import tpu as pltpu
from jax.sharding import PartitionSpec as P

RING = 4
HEADS = 8
GROUP = 4
BLOCK = 16
F32 = jnp.float32
BF16 = jnp.bfloat16


def regroup(pieces, width):
    count = pieces[0].shape[1] // width
    return [
        jnp.concatenate([piece[:, b * width : (b + 1) * width] for piece in pieces], axis=1)
        for b in range(count)
    ]


def kernel(
    logits_ref, values_ref, grads_ref, logit_grad_ref, value_grad_ref,
    raw, vals, ogs, own_grads, wts, wgs, part, core_in, xhalf, xfull, zfull, zearly, early_sum, xlate,
    stat, dots, load_sem, send_sem, recv_sem,
):
    row, col = lax.axis_index("row"), lax.axis_index("col")
    x, zh, k = row // 8, row // 2 % 4, row % 2
    y, zl = col // 2, col % 2

    def at(x=x, zh=zh, k=k, y=y, zl=zl):
        return {"row": (x % 4) * 8 + (zh % 4) * 2 + k, "col": (y % 4) * 2 + zl}

    def slot(dx=0, dz=0):
        return (x + dx + 4) % 4 * 4 + (zh + dz + 4) % 4

    def slots(dx):
        return pl.ds((x + dx + 4) % 4 * 4, 4)

    started = []

    def send(src, dst, where):
        n = len(started)
        copy = pltpu.make_async_remote_copy(
            src_ref=src, dst_ref=dst, send_sem=send_sem.at[n], recv_sem=recv_sem.at[n],
            device_id=where, device_id_type=pl.DeviceIdType.MESH,
        )
        copy.start()
        started.append(copy)
        return copy

    sibling = at(k=1 - k)
    xs = {d: at(x=x + d + 4) for d in (1, -1, 2)}
    zs = {d: at(zh=zh + d + 4) for d in (1, -1, 2)}
    ys = {d: at(y=y + d + 4) for d in (1, -1, 2)}
    twin = at(zl=1 - zl)
    cols = [{"row": row, "col": (col + d) % 8} for d in range(1, 8)]
    grads_to = at(x=y, zh=zl * 2 + x // 2, k=x % 2, y=zh, zl=1 - k)
    grads_from = at(x=zh % 2 * 2 + k, zh=y, k=1 - zl, y=x, zl=zh // 2)

    barrier = pltpu.get_barrier_semaphore()
    greeted = [grads_from, *zs.values(), *xs.values(), *cols, sibling]
    for device in greeted:
        pl.semaphore_signal(barrier, inc=1, device_id=device, device_id_type=pl.DeviceIdType.MESH)

    def load(src, dst, n):
        copy = pltpu.make_async_copy(src, dst, load_sem.at[n])
        copy.start()
        loads.append(copy)

    loads = []
    load(grads_ref, raw.at[0], HEADS)
    load(values_ref, raw.at[1], HEADS + 1)
    for h in range(HEADS):
        load(logits_ref.at[h], wts.at[h], h)
    loads[0].wait()
    for h, piece in enumerate(regroup([raw[0, s] for s in range(8)], 32)):
        own_grads[h] = piece
    loads[1].wait()
    for h, piece in enumerate(regroup([raw[1, s] for s in range(8)], 32)):
        vals[slot(), k, h] = piece
    loads = loads[2:]

    pl.semaphore_wait(barrier, len(greeted))

    groups = [pl.ds(h, GROUP) for h in range(0, HEADS, GROUP)]

    piece = zh * 2 + k
    grads_in = [send(own_grads.at[heads], ogs.at[piece, heads], grads_to) for heads in groups]

    def share(ref_slot, where, heads=None):
        ref = vals.at[ref_slot, k] if heads is None else vals.at[ref_slot, k, pl.ds(heads, 4)]
        return send(ref, ref, where)

    x_first = {0: {d: share(slot(), xs[d]) for d in (1, -1)}}
    z_first = {d: share(slot(), zs[d]) for d in (1, -1)}
    z_second = {}
    core_values = []

    lanes = lax.broadcasted_iota(jnp.int32, (128, 128), 1)
    table = jnp.zeros((128, 128), F32)

    def column(wide, h):
        return jnp.sum(jnp.where(lanes == h, wide, 0.0), axis=1, keepdims=True)

    def head_stats(h, table):
        block = wts[h]
        top = jnp.max(block, axis=1, keepdims=True)
        exponent = jnp.exp(block - top)
        wts[h] = exponent
        table = jnp.where(lanes == h, top, table)
        return jnp.where(lanes == 8 + h, jnp.sum(exponent, axis=1, keepdims=True), table)

    for load in loads:
        load.wait()
    table = lax.fori_loop(0, HEADS, head_stats, table)
    stat[col] = table.T[:16]
    stat_in = [send(stat.at[col], stat.at[col], device) for device in cols]

    mine, other = y * 2 + (1 - zl), y * 2 + zl

    def pass_on(which, heads, where):
        return send(ogs.at[which, heads], ogs.at[which, heads], where)

    twin_in, y_in = [], []
    for g, heads in enumerate(groups):
        grads_in[g].wait_recv()
        twin_in.append(pass_on(mine, heads, twin))
        y_in.append([pass_on(mine, heads, ys[d]) for d in (1, -1, 2)])

    def z_arrival(d):
        got = slot(dz=-d)
        if d == 2:
            for copy in z_second.values():
                copy.wait_recv()
        else:
            z_first[d].wait_recv()
            z_second[d] = share(got, zs[d], 0 if d == 1 else 4)
        x_first[2 if d == 2 else -d] = {e: share(got, xs[e]) for e in (1, -1)}

    x_second = []

    def share_core(dx):
        core_values.append(send(vals.at[slots(dx), k], vals.at[slots(dx), k], sibling))

    def x_arrivals(dz):
        for d in (1, -1):
            x_first[dz][d].wait_recv()
            got = slot(dx=-d, dz=dz)
            x_second.append(share(got, xs[d], 0 if d == 1 else 4))

    z_arrival(1)
    z_arrival(-1)
    x_arrivals(0)
    for g, heads in enumerate(groups):
        twin_in[g].wait_recv()
        y_in[g] += [pass_on(other, heads, ys[d]) for d in (1, -1, 2)]

    for copy in stat_in:
        copy.wait_recv()
    tops, sums = stat[:, 0:8, :], stat[:, 8:16, :]
    top = jnp.max(tops, axis=0)
    total = jnp.sum(sums * jnp.exp(tops - top[None]), axis=0)
    factor = jnp.exp(stat[col, 0:8, :] - top) / total
    factor = jnp.concatenate([factor] * 16, axis=0).T

    def scale(h, carry):
        wts[h] = wts[h] * column(factor, h)
        return carry

    lax.fori_loop(0, HEADS, scale, 0)
    z_arrival(2)
    share_core(0)


    def addend_of(h, carry):
        og = ogs[:, h].reshape(128, 256)
        addend = lax.dot_general(
            wts[h].astype(BF16), og, (((0,), (0,)), ((), ())), preferred_element_type=F32
        ).astype(BF16).reshape(4, 4, 2, BLOCK, 256)
        part[0, h] = addend[:, :, 0]
        part[1, h] = addend[:, :, 1]
        return carry

    core_sums = {}

    def addends(start, count):
        lax.fori_loop(start, start + count, addend_of, 0, unroll=True)
        heads = pl.ds(start, count)
        core_sums[start] = send(part.at[1 - k, heads], core_in.at[heads], sibling)

    order = (2, 1, -1, 0)
    place = {1: 0, -1: 1, 2: 2}
    first, second = (2, 1), (4, 2)

    def heads_of(group):
        return pl.ds(group[0], 2 * group[1])

    def half_of(group, d):
        return pl.ds(group[0] + (0 if d == 1 else group[1]), group[1])

    def held(group, d):
        return xhalf.at[place[d], pl.ds(group[0] // 2, group[1])]

    def plane(dx):
        return (x + dx + 4) % 4

    def zslot(dz):
        return (zh + dz + 4) % 4

    half_in, full_in = {}, {}

    def send_halves(group):
        for d in (1, -1):
            heads, there = half_of(group, d), plane(2)
            core_sums[half_start(group, d)].wait_recv()
            part[k, heads, there] = (
                part[k, heads, there].astype(F32) + core_in[heads, there].astype(F32)
            ).astype(BF16)
            half_in[group, d] = send(part.at[k, heads, there], held(group, d), xs[d])

    def half_start(group, d):
        return group[0] + (0 if d == 1 else group[1])

    def send_fulls(group):
        for d in (1, -1):
            heads, there = half_of(group, -d), plane(d)
            part[k, heads, there] = (
                part[k, heads, there].astype(F32) + core_in[heads, there].astype(F32)
            ).astype(BF16)
        for d in (1, -1):
            heads, there = half_of(group, d), plane(d)
            half_in[group, d].wait_recv()
            part[k, heads, there] = (
                part[k, heads, there].astype(F32) + core_in[heads, there].astype(F32)
                + held(group, d)[...].astype(F32)
            ).astype(BF16)
            for dz in order:
                full_in[group, dz, d] = send(
                    part.at[k, heads_of(group), there, zslot(dz)],
                    xfull.at[place[d], heads_of(group), zslot(dz)], xs[d],
                )

    def arrived(group, dz):
        heads, here = heads_of(group), zslot(dz)
        total = part[k, heads, x, here].astype(F32) + core_in[heads, x, here].astype(F32)
        for d in (1, -1):
            full_in[group, dz, d].wait_recv()
            total += xfull[place[d], heads, here].astype(F32)
        return total

    z_full = {}

    def send_on(group):
        heads = heads_of(group)
        for dz in (2, 1, -1):
            here = zslot(dz)
            part[k, heads, x, here] = arrived(group, dz).astype(BF16)
            z_full[group, dz] = send(part.at[k, heads, x, here], zfull.at[place[dz], heads], zs[dz])

    z_early, x_late = {}, {}

    def send_early():
        heads = pl.ds(0, 2)
        core_sums[0].wait_recv()
        for dz in (2, 1, -1):
            here = zslot(dz)
            part[k, heads, :, here] = (
                part[k, heads, :, here].astype(F32) + core_in[heads, :, here].astype(F32)
            ).astype(BF16)
            z_early[dz] = send(part.at[k, heads, :, here], zearly.at[place[dz]], zs[dz])

    def send_late():
        heads = pl.ds(0, 2)
        total = part[k, heads, :, zh].astype(F32) + core_in[heads, :, zh].astype(F32)
        for dz in (2, 1, -1):
            z_early[dz].wait_recv()
            total += zearly[place[dz]].astype(F32)
        early_sum[...] = total.astype(BF16)
        for dx in (2, 1, -1):
            x_late[dx] = send(early_sum.at[:, plane(dx)], xlate.at[place[dx]], xs[dx])

    x_arrivals(1)
    x_arrivals(-1)
    for copy in y_in[0]:
        copy.wait_recv()
    addends(2, 1)
    addends(3, 1)
    addends(0, 2)
    send_halves(first)
    send_early()
    x_arrivals(2)
    share_core(1)
    share_core(-1)
    for copy in y_in[1]:
        copy.wait_recv()
    addends(4, 2)
    addends(6, 2)
    send_halves(second)

    send_fulls(first)
    send_fulls(second)
    for copy in x_second:
        copy.wait_recv()
    share_core(2)
    send_on(first)

    for copy in core_values:
        copy.wait_recv()
    table = jnp.zeros((128, 128), F32)

    def weight_grads(h, table):
        weight_grad = lax.dot_general(
            ogs[:, h].reshape(128, 256), vals[:, :, h].reshape(512, 256),
            (((1,), (1,)), ((), ())), preferred_element_type=F32,
        )
        wgs[h] = weight_grad
        return jnp.where(lanes == h, jnp.sum(weight_grad * wts[h], axis=1, keepdims=True), table)

    for h in range(HEADS):
        table = weight_grads(h, table)
    dots[col] = table.T[:8]
    dot_in = [send(dots.at[col], dots.at[col], device) for device in cols]
    send_late()

    send_on(second)

    for copy in dot_in:
        copy.wait_recv()
    row_dot = jnp.sum(dots[...], axis=0)
    row_dot = jnp.concatenate([row_dot] * 16, axis=0).T

    for h in range(HEADS):
        logit_grad_ref[h] = wts[h] * (wgs[h] - row_dot[:, h : h + 1])

    early = early_sum[:, x].astype(F32)
    for dx in (2, 1, -1):
        x_late[dx].wait_recv()
        early += xlate[place[dx]].astype(F32)
    totals = [early[0], early[1]]
    for group in (first, second):
        total = arrived(group, 0)
        for dz in (2, 1, -1):
            z_full[group, dz].wait_recv()
            total += zfull[place[dz], heads_of(group)].astype(F32)
        totals += [total[h] for h in range(2 * group[1])]
    for s, piece in enumerate(regroup(totals, 32)):
        value_grad_ref[s] = piece.astype(BF16)

    for copy in started:
        copy.wait_send()


def store(logit_grad, value_grad, logit_grad_ref, value_grad_ref, sem):
    copies = [
        pltpu.make_async_copy(logit_grad, logit_grad_ref, sem.at[0]),
        pltpu.make_async_copy(value_grad, value_grad_ref, sem.at[1]),
    ]
    for copy in copies:
        copy.start()
    for copy in copies:
        copy.wait()


def per_device(logits, values, output_gradient):
    vmem = pl.BlockSpec(memory_space=pltpu.VMEM)
    hbm = pl.BlockSpec(memory_space=pltpu.HBM)
    copies = 136
    outs = (jax.ShapeDtypeStruct(logits.shape, F32), jax.ShapeDtypeStruct(values.shape, BF16))
    results = pl.pallas_call(
        kernel,
        out_shape=outs,
        in_specs=[hbm] * 3,
        out_specs=(vmem, vmem),
        scratch_shapes=[
            pltpu.VMEM((2, 8, BLOCK, 256), BF16),
            pltpu.VMEM((16, 2, HEADS, BLOCK, 256), BF16),
            pltpu.VMEM((8, HEADS, BLOCK, 256), BF16),
            pltpu.VMEM((HEADS, BLOCK, 256), BF16),
            pltpu.VMEM((HEADS, 128, 512), F32),
            pltpu.VMEM((HEADS, 128, 512), F32),
            pltpu.VMEM((2, HEADS, RING, RING, BLOCK, 256), BF16),
            pltpu.VMEM((HEADS, RING, RING, BLOCK, 256), BF16),
            pltpu.VMEM((2, 4, RING, BLOCK, 256), BF16),
            pltpu.VMEM((2, HEADS, RING, BLOCK, 256), BF16),
            pltpu.VMEM((3, HEADS, BLOCK, 256), BF16),
            pltpu.VMEM((3, 2, RING, BLOCK, 256), BF16),
            pltpu.VMEM((2, RING, BLOCK, 256), BF16),
            pltpu.VMEM((3, 2, BLOCK, 256), BF16),
            pltpu.VMEM((8, 16, 128), F32),
            pltpu.VMEM((8, 8, 128), F32),
            pltpu.SemaphoreType.DMA((HEADS + 2,)),
            pltpu.SemaphoreType.DMA((copies,)),
            pltpu.SemaphoreType.DMA((copies,)),
        ],
        compiler_params=pltpu.CompilerParams(
            collective_id=0, has_side_effects=True, vmem_limit_bytes=40 * 1024 * 1024
        ),
    )(*(pltpu.with_memory_space_constraint(a, pltpu.HBM) for a in (logits, values, output_gradient)))
    return pl.pallas_call(
        store,
        out_shape=outs,
        in_specs=[pl.BlockSpec(memory_space=pl.ANY)] * 2,
        out_specs=(hbm, hbm),
        scratch_shapes=[pltpu.SemaphoreType.DMA((2,))],
        compiler_params=pltpu.CompilerParams(vmem_limit_bytes=1024 * 1024),
    )(*results)


def solution(mesh):
    placed = (P(None, "row", "col"), P(None, ("col", "row"), None), P(None, ("col", "row"), None))
    return jax.shard_map(
        per_device,
        mesh=mesh,
        in_specs=placed,
        out_specs=(P(None, "row", "col"), P(None, ("col", "row"), None)),
        check_vma=False,
    )
```

```python
import functools

import jax
import jax.numpy as jnp
from jax import lax
from jax.experimental import pallas as pl
from jax.experimental.pallas import tpu as pltpu
from jax.sharding import PartitionSpec as P

RING = 4
HEADS = 8
GROUP = 4
BLOCK = 16
F32 = jnp.float32
BF16 = jnp.bfloat16


def regroup(pieces, width):
    count = pieces[0].shape[1] // width
    return [
        jnp.concatenate([piece[:, b * width : (b + 1) * width] for piece in pieces], axis=1)
        for b in range(count)
    ]


def kernel(
    logits_ref, values_ref, grads_ref, logit_grad_ref, value_grad_ref,
    raw, vals, ogs, own_grads, wts, wgs, part, core_in, xhalf, xfull, zfull, zearly, early_sum, xlate,
    stat, dots, load_sem, send_sem, recv_sem,
):
    row, col = lax.axis_index("row"), lax.axis_index("col")
    x, zh, k = row // 8, row // 2 % 4, row % 2
    y, zl = col // 2, col % 2

    def at(x=x, zh=zh, k=k, y=y, zl=zl):
        return {"row": (x % 4) * 8 + (zh % 4) * 2 + k, "col": (y % 4) * 2 + zl}

    def slot(dx=0, dz=0):
        return (x + dx + 4) % 4 * 4 + (zh + dz + 4) % 4

    def slots(dx):
        return pl.ds((x + dx + 4) % 4 * 4, 4)

    started = []

    def send(src, dst, where):
        n = len(started)
        copy = pltpu.make_async_remote_copy(
            src_ref=src, dst_ref=dst, send_sem=send_sem.at[n], recv_sem=recv_sem.at[n],
            device_id=where, device_id_type=pl.DeviceIdType.MESH,
        )
        copy.start()
        started.append(copy)
        return copy

    sibling = at(k=1 - k)
    xs = {d: at(x=x + d + 4) for d in (1, -1, 2)}
    zs = {d: at(zh=zh + d + 4) for d in (1, -1, 2)}
    ys = {d: at(y=y + d + 4) for d in (1, -1, 2)}
    twin = at(zl=1 - zl)
    cols = [{"row": row, "col": (col + d) % 8} for d in range(1, 8)]
    grads_to = at(x=y, zh=zl * 2 + x // 2, k=x % 2, y=zh, zl=1 - k)
    grads_from = at(x=zh % 2 * 2 + k, zh=y, k=1 - zl, y=x, zl=zh // 2)

    barrier = pltpu.get_barrier_semaphore()
    greeted = [grads_from, *zs.values(), *xs.values(), *cols, sibling]
    for device in greeted:
        pl.semaphore_signal(barrier, inc=1, device_id=device, device_id_type=pl.DeviceIdType.MESH)

    def load(src, dst, n):
        copy = pltpu.make_async_copy(src, dst, load_sem.at[n])
        copy.start()
        loads.append(copy)

    loads = []
    load(grads_ref, raw.at[0], HEADS)
    load(values_ref, raw.at[1], HEADS + 1)
    for h in range(HEADS):
        load(logits_ref.at[h], wts.at[h], h)
    loads[0].wait()
    for h, piece in enumerate(regroup([raw[0, s] for s in range(8)], 32)):
        own_grads[h] = piece
    loads[1].wait()
    for h, piece in enumerate(regroup([raw[1, s] for s in range(8)], 32)):
        vals[slot(), k, h] = piece
    loads = loads[2:]

    pl.semaphore_wait(barrier, len(greeted))

    groups = [pl.ds(h, GROUP) for h in range(0, HEADS, GROUP)]

    piece = zh * 2 + k
    grads_in = [send(own_grads.at[heads], ogs.at[piece, heads], grads_to) for heads in groups]

    def share(ref_slot, where, heads=None):
        ref = vals.at[ref_slot, k] if heads is None else vals.at[ref_slot, k, pl.ds(heads, 4)]
        return send(ref, ref, where)

    x_first = {0: {d: share(slot(), xs[d]) for d in (1, -1)}}
    z_first = {d: share(slot(), zs[d]) for d in (1, -1)}
    z_second = {}
    core_values = []

    lanes = lax.broadcasted_iota(jnp.int32, (128, 128), 1)
    table = jnp.zeros((128, 128), F32)

    def column(wide, h):
        return jnp.sum(jnp.where(lanes == h, wide, 0.0), axis=1, keepdims=True)

    def head_stats(h, table):
        block = wts[h]
        top = jnp.max(block, axis=1, keepdims=True)
        exponent = jnp.exp(block - top)
        wts[h] = exponent
        table = jnp.where(lanes == h, top, table)
        return jnp.where(lanes == 8 + h, jnp.sum(exponent, axis=1, keepdims=True), table)

    for load in loads:
        load.wait()
    table = lax.fori_loop(0, HEADS, head_stats, table)
    stat[col] = table.T[:16]
    stat_in = [send(stat.at[col], stat.at[col], device) for device in cols]

    mine, other = y * 2 + (1 - zl), y * 2 + zl

    def pass_on(which, heads, where):
        return send(ogs.at[which, heads], ogs.at[which, heads], where)

    twin_in, y_in = [], []
    for g, heads in enumerate(groups):
        grads_in[g].wait_recv()
        twin_in.append(pass_on(mine, heads, twin))
        y_in.append([pass_on(mine, heads, ys[d]) for d in (1, -1, 2)])

    def z_arrival(d):
        got = slot(dz=-d)
        if d == 2:
            for copy in z_second.values():
                copy.wait_recv()
        else:
            z_first[d].wait_recv()
            z_second[d] = share(got, zs[d], 0 if d == 1 else 4)
        x_first[2 if d == 2 else -d] = {e: share(got, xs[e]) for e in (1, -1)}

    x_second = []

    def share_core(dx):
        core_values.append(send(vals.at[slots(dx), k], vals.at[slots(dx), k], sibling))

    def x_arrivals(dz):
        for d in (1, -1):
            x_first[dz][d].wait_recv()
            got = slot(dx=-d, dz=dz)
            x_second.append(share(got, xs[d], 0 if d == 1 else 4))

    z_arrival(1)
    z_arrival(-1)
    x_arrivals(0)
    for g, heads in enumerate(groups):
        twin_in[g].wait_recv()
        y_in[g] += [pass_on(other, heads, ys[d]) for d in (1, -1, 2)]

    for copy in stat_in:
        copy.wait_recv()
    tops, sums = stat[:, 0:8, :], stat[:, 8:16, :]
    top = jnp.max(tops, axis=0)
    total = jnp.sum(sums * jnp.exp(tops - top[None]), axis=0)
    factor = jnp.exp(stat[col, 0:8, :] - top) / total
    factor = jnp.concatenate([factor] * 16, axis=0).T

    def scale(h, carry):
        wts[h] = wts[h] * column(factor, h)
        return carry

    lax.fori_loop(0, HEADS, scale, 0)
    z_arrival(2)
    share_core(0)


    def addend_of(h, carry):
        og = ogs[:, h].reshape(128, 256)
        addend = lax.dot_general(
            wts[h].astype(BF16), og, (((0,), (0,)), ((), ())), preferred_element_type=F32
        ).astype(BF16).reshape(4, 4, 2, BLOCK, 256)
        part[0, h] = addend[:, :, 0]
        part[1, h] = addend[:, :, 1]
        return carry

    core_sums = {}

    def addends(start, count):
        lax.fori_loop(start, start + count, addend_of, 0, unroll=True)
        heads = pl.ds(start, count)
        core_sums[start] = send(part.at[1 - k, heads], core_in.at[heads], sibling)

    order = (2, 1, -1, 0)
    place = {1: 0, -1: 1, 2: 2}
    first, second = (2, 1), (4, 2)

    def heads_of(group):
        return pl.ds(group[0], 2 * group[1])

    def half_of(group, d):
        return pl.ds(group[0] + (0 if d == 1 else group[1]), group[1])

    def held(group, d):
        return xhalf.at[place[d], pl.ds(group[0] // 2, group[1])]

    def plane(dx):
        return (x + dx + 4) % 4

    def zslot(dz):
        return (zh + dz + 4) % 4

    half_in, full_in = {}, {}

    def send_halves(group):
        for d in (1, -1):
            heads, there = half_of(group, d), plane(2)
            core_sums[half_start(group, d)].wait_recv()
            part[k, heads, there] = (
                part[k, heads, there].astype(F32) + core_in[heads, there].astype(F32)
            ).astype(BF16)
            half_in[group, d] = send(part.at[k, heads, there], held(group, d), xs[d])

    def half_start(group, d):
        return group[0] + (0 if d == 1 else group[1])

    def send_fulls(group):
        for d in (1, -1):
            heads, there = half_of(group, -d), plane(d)
            part[k, heads, there] = (
                part[k, heads, there].astype(F32) + core_in[heads, there].astype(F32)
            ).astype(BF16)
        for d in (1, -1):
            heads, there = half_of(group, d), plane(d)
            half_in[group, d].wait_recv()
            part[k, heads, there] = (
                part[k, heads, there].astype(F32) + core_in[heads, there].astype(F32)
                + held(group, d)[...].astype(F32)
            ).astype(BF16)
            for dz in order:
                full_in[group, dz, d] = send(
                    part.at[k, heads_of(group), there, zslot(dz)],
                    xfull.at[place[d], heads_of(group), zslot(dz)], xs[d],
                )

    def arrived(group, dz):
        heads, here = heads_of(group), zslot(dz)
        total = part[k, heads, x, here].astype(F32) + core_in[heads, x, here].astype(F32)
        for d in (1, -1):
            full_in[group, dz, d].wait_recv()
            total += xfull[place[d], heads, here].astype(F32)
        return total

    z_full = {}

    def send_on(group):
        heads = heads_of(group)
        for dz in (2, 1, -1):
            here = zslot(dz)
            part[k, heads, x, here] = arrived(group, dz).astype(BF16)
            z_full[group, dz] = send(part.at[k, heads, x, here], zfull.at[place[dz], heads], zs[dz])

    z_early, x_late = {}, {}

    def send_early():
        heads = pl.ds(0, 2)
        core_sums[0].wait_recv()
        for dz in (2, 1, -1):
            here = zslot(dz)
            part[k, heads, :, here] = (
                part[k, heads, :, here].astype(F32) + core_in[heads, :, here].astype(F32)
            ).astype(BF16)
            z_early[dz] = send(part.at[k, heads, :, here], zearly.at[place[dz]], zs[dz])

    def send_late():
        heads = pl.ds(0, 2)
        total = part[k, heads, :, zh].astype(F32) + core_in[heads, :, zh].astype(F32)
        for dz in (2, 1, -1):
            z_early[dz].wait_recv()
            total += zearly[place[dz]].astype(F32)
        early_sum[...] = total.astype(BF16)
        for dx in (2, 1, -1):
            x_late[dx] = send(early_sum.at[:, plane(dx)], xlate.at[place[dx]], xs[dx])

    x_arrivals(1)
    x_arrivals(-1)
    for copy in y_in[0]:
        copy.wait_recv()
    addends(2, 1)
    addends(3, 1)
    addends(0, 2)
    send_halves(first)
    send_early()
    x_arrivals(2)
    share_core(1)
    share_core(-1)
    for copy in y_in[1]:
        copy.wait_recv()
    addends(4, 2)
    addends(6, 2)
    send_halves(second)

    send_fulls(first)
    for copy in x_second:
        copy.wait_recv()
    share_core(2)
    send_fulls(second)
    send_on(first)

    for copy in core_values:
        copy.wait_recv()
    table = jnp.zeros((128, 128), F32)

    def weight_grads(h, table):
        weight_grad = lax.dot_general(
            ogs[:, h].reshape(128, 256), vals[:, :, h].reshape(512, 256),
            (((1,), (1,)), ((), ())), preferred_element_type=F32,
        )
        wgs[h] = weight_grad
        return jnp.where(lanes == h, jnp.sum(weight_grad * wts[h], axis=1, keepdims=True), table)

    for h in range(HEADS):
        table = weight_grads(h, table)
    dots[col] = table.T[:8]
    dot_in = [send(dots.at[col], dots.at[col], device) for device in cols]
    send_late()

    send_on(second)

    for copy in dot_in:
        copy.wait_recv()
    row_dot = jnp.sum(dots[...], axis=0)
    row_dot = jnp.concatenate([row_dot] * 16, axis=0).T

    for h in range(HEADS):
        logit_grad_ref[h] = wts[h] * (wgs[h] - row_dot[:, h : h + 1])

    early = early_sum[:, x].astype(F32)
    for dx in (2, 1, -1):
        x_late[dx].wait_recv()
        early += xlate[place[dx]].astype(F32)
    totals = [early[0], early[1]]
    for group in (first, second):
        total = arrived(group, 0)
        for dz in (2, 1, -1):
            z_full[group, dz].wait_recv()
            total += zfull[place[dz], heads_of(group)].astype(F32)
        totals += [total[h] for h in range(2 * group[1])]
    for s, piece in enumerate(regroup(totals, 32)):
        value_grad_ref[s] = piece.astype(BF16)

    for copy in started:
        copy.wait_send()


def store(logit_grad, value_grad, logit_grad_ref, value_grad_ref, sem):
    copies = [
        pltpu.make_async_copy(logit_grad, logit_grad_ref, sem.at[0]),
        pltpu.make_async_copy(value_grad, value_grad_ref, sem.at[1]),
    ]
    for copy in copies:
        copy.start()
    for copy in copies:
        copy.wait()


def per_device(logits, values, output_gradient):
    vmem = pl.BlockSpec(memory_space=pltpu.VMEM)
    hbm = pl.BlockSpec(memory_space=pltpu.HBM)
    copies = 136
    outs = (jax.ShapeDtypeStruct(logits.shape, F32), jax.ShapeDtypeStruct(values.shape, BF16))
    results = pl.pallas_call(
        kernel,
        out_shape=outs,
        in_specs=[hbm] * 3,
        out_specs=(vmem, vmem),
        scratch_shapes=[
            pltpu.VMEM((2, 8, BLOCK, 256), BF16),
            pltpu.VMEM((16, 2, HEADS, BLOCK, 256), BF16),
            pltpu.VMEM((8, HEADS, BLOCK, 256), BF16),
            pltpu.VMEM((HEADS, BLOCK, 256), BF16),
            pltpu.VMEM((HEADS, 128, 512), F32),
            pltpu.VMEM((HEADS, 128, 512), F32),
            pltpu.VMEM((2, HEADS, RING, RING, BLOCK, 256), BF16),
            pltpu.VMEM((HEADS, RING, RING, BLOCK, 256), BF16),
            pltpu.VMEM((2, 4, RING, BLOCK, 256), BF16),
            pltpu.VMEM((2, HEADS, RING, BLOCK, 256), BF16),
            pltpu.VMEM((3, HEADS, BLOCK, 256), BF16),
            pltpu.VMEM((3, 2, RING, BLOCK, 256), BF16),
            pltpu.VMEM((2, RING, BLOCK, 256), BF16),
            pltpu.VMEM((3, 2, BLOCK, 256), BF16),
            pltpu.VMEM((8, 16, 128), F32),
            pltpu.VMEM((8, 8, 128), F32),
            pltpu.SemaphoreType.DMA((HEADS + 2,)),
            pltpu.SemaphoreType.DMA((copies,)),
            pltpu.SemaphoreType.DMA((copies,)),
        ],
        compiler_params=pltpu.CompilerParams(
            collective_id=0, has_side_effects=True, vmem_limit_bytes=40 * 1024 * 1024
        ),
    )(*(pltpu.with_memory_space_constraint(a, pltpu.HBM) for a in (logits, values, output_gradient)))
    return pl.pallas_call(
        store,
        out_shape=outs,
        in_specs=[pl.BlockSpec(memory_space=pl.ANY)] * 2,
        out_specs=(hbm, hbm),
        scratch_shapes=[pltpu.SemaphoreType.DMA((2,))],
        compiler_params=pltpu.CompilerParams(vmem_limit_bytes=1024 * 1024),
    )(*results)


def solution(mesh):
    placed = (P(None, "row", "col"), P(None, ("col", "row"), None), P(None, ("col", "row"), None))
    return jax.shard_map(
        per_device,
        mesh=mesh,
        in_specs=placed,
        out_specs=(P(None, "row", "col"), P(None, ("col", "row"), None)),
        check_vma=False,
    )
```
